32 devices in a mesh: groups: 2 (over y), blk: 4 (over z), sub: 2 (over x), pair: 2 (over core).
Axes of the slice: x: 2, y: 2, z: 4, core: 2. Of those that a mesh axis runs over, the one named last changes fastest.
Arguments:
- source: bfloat16 [8, 2048, 256], P(('groups', 'blk'), 'sub'), parts along dimension 0, may hold values from -0.5 to 0.5
- target: bfloat16 [64, 512, 256], P(('groups', 'blk'), 'pair'), parts along dimension 0, may hold values from -0.5 to 0.5
- target_slot_index: int32 [64], P('groups'), parts along dimension 0, may hold values from 0 to 31, as said below
- active_block_table: int32 [8, 16], P('groups'), parts along dimension 0, may hold values from -1 to 31, as said below
- active_count: int32 [8], P('groups'), parts along dimension 0, may hold values from 10 to 16, as said below
Outputs:
- row_potential: float32 [8, 2048], P(('groups', 'blk'), 'sub'), parts along dimension 0
- column_potential: float32 [64, 512], P(('groups', 'blk'), 'pair'), parts along dimension 0
The draws below stay inside these ranges and needn't reach their ends.
There are 2 independent parts, one for each index of `groups`. The reference program is written for one: setup_inputs(seed, part) draws one part's arguments, and reference() takes and returns one part's arrays. A program takes and returns all parts, laid end to end along the dimension named above; each array names one. Nothing has to cross between parts.
Inputs may be any that keep to these rules, and one draw needn't show every extreme that they name: `target_slot_index`: A permutation: slots o * 8 to (o + 1) * 8 - 1 are those of owner o along blk. `active_block_table`: the first active_count[r] entries of row r are distinct target blocks, the rest are -1; in every row at most 8 live entries lie in slots of one owner, and some owner holds exactly 8 of them. `active_count`: some row block has 16 live entries.
All inputs are finite; a program needn't handle non-finite values.
Results may differ from the reference program's by a relative error of at most 0.0003.
Values may be sent and summed in bfloat16 or wider, within the bound.
A program may use at most 128 MiB of HBM per device.

```python
import math
import jax
import jax.numpy as jnp
from jax import lax

D = 256
RB = 2048
TB = 512
K = 16
TPD = 8
ITERS = 3
NRB = 4
NTB = 32
CAP = 8


def layout(key):
    permuted = jax.random.permutation(jax.random.fold_in(key, 101), NTB).astype(jnp.int32)
    inverse = jnp.argsort(permuted).astype(jnp.int32)
    lowest = 5 * K // 8
    counts = jax.random.randint(jax.random.fold_in(key, 102), (NRB,), lowest, K + 1)
    chosen_full = jax.random.randint(jax.random.fold_in(key, 103), (), 0, NRB)
    block_ids = jnp.arange(NRB, dtype=jnp.int32)
    counts = jnp.where(block_ids == (chosen_full + 1) % NRB, lowest, counts)
    counts = jnp.where(block_ids == chosen_full, K, counts).astype(jnp.int32)
    items = NRB * CAP
    element_index = jnp.arange(items, dtype=jnp.int32)
    item_owner = element_index // CAP
    noise = jax.random.randint(jax.random.fold_in(key, 104), (NRB, items), 0, 1 << 20)
    forced = item_owner[None, :] == block_ids[:, None]
    ranking = jnp.where(forced, element_index[None, :], (noise + 1) * items + element_index[None, :])
    order = jnp.argsort(ranking, axis=1)[:, :K].astype(jnp.int32)
    shifts = jax.random.randint(jax.random.fold_in(key, 105), (NRB, NRB), 0, TPD)
    chosen_owner = order // CAP
    chosen_copy = order % CAP
    chosen_shift = jnp.take_along_axis(shifts, chosen_owner, axis=1)
    slots = chosen_owner * TPD + (chosen_shift + chosen_copy) % TPD
    ids = jnp.take(inverse, slots, axis=0)
    lists = jnp.where(jnp.arange(K, dtype=jnp.int32)[None, :] < counts[:, None], ids, -1)
    return (permuted, lists.astype(jnp.int32), counts)


def embeddings(key, array_extent):
    values = jnp.clip(jax.random.normal(key, array_extent, jnp.float32), -6.0, 6.0)
    return jnp.clip(values / math.sqrt(D), -0.5, 0.5).astype(jnp.bfloat16)


def draw_source(key, part):
    key = jax.random.fold_in(key, 1)
    return embeddings(key, (NRB, RB, D))


def draw_target(key, part):
    key = jax.random.fold_in(key, 2)
    return embeddings(key, (NTB, TB, D))


def draw_target_slot_index(key, part):
    return layout(key)[0]


def draw_active_block_table(key, part):
    return layout(key)[1]


def draw_active_count(key, part):
    return layout(key)[2]


def setup_inputs(seed: int = 0, part: int = 0) -> dict:
    key_list = jax.random.split(jax.random.key(seed), 6)
    part_splits = jax.random.split(jax.random.fold_in(key_list[5], part), 6)
    return {
        "source": draw_source(jax.random.fold_in(jax.random.fold_in(key_list[5], part), 71), part),
        "target": draw_target(jax.random.fold_in(jax.random.fold_in(key_list[5], part), 71), part),
        "target_slot_index": draw_target_slot_index(jax.random.fold_in(jax.random.fold_in(key_list[5], part), 71), part),
        "active_block_table": draw_active_block_table(jax.random.fold_in(jax.random.fold_in(key_list[5], part), 71), part),
        "active_count": draw_active_count(jax.random.fold_in(jax.random.fold_in(key_list[5], part), 71), part),
    }


EPSILON = 0.01
FLOOR_VALUE = -1.0e30


def block_cost(source_block, half_row, target_wide, half_target, slot_row):
    picked = jnp.take(target_wide, slot_row, axis=0)
    cross_term = jnp.einsum("id,kjd->ikj", source_block, picked, precision=lax.Precision.HIGHEST)
    return half_row[:, None, None] + jnp.take(half_target, slot_row, axis=0)[None] - cross_term


def reference(source, target, target_slot_index, active_block_table, active_count):
    list_length = active_block_table.shape[1]
    live_mask = jnp.arange(list_length, dtype=jnp.int32)[None, :] < active_count[:, None]
    slot_table = jnp.take(target_slot_index, jnp.maximum(active_block_table, 0), axis=0).astype(jnp.int32)
    source_wide = source.astype(jnp.float32)
    target_wide = target.astype(jnp.float32)
    half_source = 0.5 * jnp.sum(jnp.square(source_wide), axis=2)
    half_target = 0.5 * jnp.sum(jnp.square(target_wide), axis=2)
    block_ids = jnp.arange(source.shape[0], dtype=jnp.int32)
    slot_ids = jnp.arange(target.shape[0], dtype=jnp.int32)
    column_potential = jnp.zeros(target.shape[:2], jnp.float32)
    row_potential = jnp.zeros(source.shape[:2], jnp.float32)
    flat_slots = slot_table.reshape(-1)
    flat_live = live_mask.reshape(-1)
    for iteration in range(ITERS):
        def row_update(block_index):
            slot_row = slot_table[block_index]
            cost = block_cost(source_wide[block_index], half_source[block_index], target_wide, half_target, slot_row)
            scores = (jnp.take(column_potential, slot_row, axis=0)[None] - cost) / EPSILON
            scores = jnp.where(live_mask[block_index][None, :, None], scores, FLOOR_VALUE)
            peak = jnp.max(scores, axis=(1, 2))
            mass = jnp.sum(jnp.exp(scores - peak[:, None, None]), axis=(1, 2))
            return -EPSILON * (peak + jnp.log(mass))

        row_potential = lax.map(row_update, block_ids)

        def column_part(block_index):
            slot_row = slot_table[block_index]
            cost = block_cost(source_wide[block_index], half_source[block_index], target_wide, half_target, slot_row)
            scores = (row_potential[block_index][:, None, None] - cost) / EPSILON
            peak = jnp.max(scores, axis=0)
            mass = jnp.sum(jnp.exp(scores - peak[None]), axis=0)
            return peak, mass

        peaks, masses = lax.map(column_part, block_ids)
        flat_peaks = peaks.reshape(-1, peaks.shape[2])
        flat_masses = masses.reshape(-1, masses.shape[2])

        def column_update(slot_index):
            slot_hit = flat_live & (flat_slots == slot_index)
            best_peak = jnp.max(jnp.where(slot_hit[:, None], flat_peaks, FLOOR_VALUE), axis=0)
            weight = jnp.sum(jnp.where(slot_hit[:, None], flat_masses * jnp.exp(flat_peaks - best_peak[None]), 0.0), axis=0)
            is_named = jnp.any(slot_hit)
            return jnp.where(is_named, -EPSILON * (best_peak + jnp.log(jnp.where(is_named, weight, 1.0))), 0.0)

        column_potential = lax.map(column_update, slot_ids)
    return row_potential, column_potential
```

```python
import functools
import math

import jax
import jax.numpy as jnp
from jax import lax
from jax.experimental import pallas as pl
from jax.experimental.pallas import tpu as pltpu
from jax.sharding import PartitionSpec as P

ITERS = 3
EPSILON = 0.01
FLOOR_VALUE = -1e30
TO_BITS = 1.0 / (EPSILON * math.log(2.0))
FROM_BITS = EPSILON * math.log(2.0)
MESH = pl.DeviceIdType.MESH
LIMIT = 48 * 1024 * 1024
VMEM = pltpu.VMEM


def vspec():
    return pl.BlockSpec(memory_space=pltpu.VMEM)


def sspec():
    return pl.BlockSpec(memory_space=pltpu.SMEM)


def log_join(peak, mass):
    safe = jnp.where(mass > 0.0, mass, 1.0)
    return jnp.where(mass > 0.0, peak + FROM_BITS * jnp.log2(safe), FLOOR_VALUE)


def log_sum(parts):
    peak = functools.reduce(jnp.maximum, parts)
    mass = functools.reduce(jnp.add, [jnp.exp2((p - peak) * TO_BITS) for p in parts])
    return peak + FROM_BITS * jnp.log2(mass)


def collapse(peak, mass):
    top = jnp.max(peak, axis=0, keepdims=True)
    total = jnp.sum(mass * jnp.exp2((peak - top) * TO_BITS), axis=0, keepdims=True)
    return log_join(top, total)


def gather_kernel(blocks, s_ref, all_ref, up_send, up_recv, down_send, down_recv, pair_send, pair_recv, own_sem):
    z = lax.axis_index("blk")
    c = lax.axis_index("pair")
    rows = s_ref.shape[0]
    half = rows // 2
    mine = pl.ds(pl.multiple_of(c * half, half), half)
    barrier = pltpu.get_barrier_semaphore()
    has_up = z + 1 < blocks
    has_down = z > 0

    @pl.when(has_up)
    def _():
        pl.semaphore_signal(barrier, inc=1, device_id={"blk": z + 1}, device_id_type=MESH)

    @pl.when(has_down)
    def _():
        pl.semaphore_signal(barrier, inc=1, device_id={"blk": z - 1}, device_id_type=MESH)

    pl.semaphore_signal(barrier, inc=1, device_id={"pair": 1 - c}, device_id_type=MESH)
    pl.semaphore_wait(barrier, 1 + has_up.astype(jnp.int32) + has_down.astype(jnp.int32))

    def hop(block, step, target, send, recv, first):
        return pltpu.make_async_remote_copy(
            src_ref=s_ref.at[mine] if first else all_ref.at[block, mine],
            dst_ref=all_ref.at[block, mine],
            send_sem=send.at[step],
            recv_sem=recv.at[step],
            device_id={"blk": target},
            device_id_type=MESH,
        )

    def across(block, slot):
        return pltpu.make_async_remote_copy(
            src_ref=all_ref.at[block, mine],
            dst_ref=all_ref.at[block, mine],
            send_sem=pair_send.at[slot],
            recv_sem=pair_recv.at[slot],
            device_id={"pair": 1 - c},
            device_id_type=MESH,
        )

    own = pltpu.make_async_copy(s_ref, all_ref.at[z], own_sem)
    own.start()

    @pl.when(has_up)
    def _():
        hop(z, 0, z + 1, up_send, up_recv, True).start()

    @pl.when(has_down)
    def _():
        hop(z, 0, z - 1, down_send, down_recv, True).start()

    for step in range(blocks - 1):
        below = z - 1 - step
        above = z + 1 + step

        @pl.when(below >= 0)
        def _():
            hop(below, step, z, up_send, up_recv, False).wait_recv()

            @pl.when(has_up)
            def _():
                hop(below, step + 1, z + 1, up_send, up_recv, False).start()

            across(below, below).start()

        @pl.when(above < blocks)
        def _():
            hop(above, step, z, down_send, down_recv, False).wait_recv()

            @pl.when(has_down)
            def _():
                hop(above, step + 1, z - 1, down_send, down_recv, False).start()

            across(above, above).start()

    own.wait()
    for block in range(blocks):

        @pl.when(block != z)
        def _():
            across(block, block).wait()

    for step in range(blocks):

        @pl.when(has_up & (z - step >= 0))
        def _():
            hop(z, step, z + 1, up_send, up_recv, True).wait_send()

        @pl.when(has_down & (z + step < blocks))
        def _():
            hop(z, step, z - 1, down_send, down_recv, True).wait_send()


def gather_rows(source, blocks):
    return pl.pallas_call(
        functools.partial(gather_kernel, blocks),
        out_shape=jax.ShapeDtypeStruct((blocks,) + source.shape, source.dtype),
        in_specs=[vspec()],
        out_specs=vspec(),
        scratch_shapes=[pltpu.SemaphoreType.DMA((blocks,)) for _ in range(6)]
        + [pltpu.SemaphoreType.DMA],
        compiler_params=pltpu.CompilerParams(
            collective_id=0, has_side_effects=True, vmem_limit_bytes=LIMIT
        ),
        name="gather_rows",
    )(source)


def tile_of(rows):
    return 256 if rows % 256 == 0 else rows


def absorb(scores, peak, mass, at):
    parts = scores.reshape(scores.shape[0] // 8, 8, scores.shape[1])
    old = peak[at]
    new = jnp.maximum(old, jnp.max(parts, axis=0))
    peak[at] = new
    mass[at] = mass[at] * jnp.exp2((old - new) * TO_BITS) + jnp.sum(
        jnp.exp2((parts - new[None]) * TO_BITS), axis=0
    )


def row_kernel(live, s_ref, t_ref, g_ref, out, peak, mass, spread):
    blocks, rows, depth = s_ref.shape
    slots, points, _ = t_ref.shape
    tile = tile_of(rows)
    peak[...] = jnp.full(peak.shape, FLOOR_VALUE, jnp.float32)
    mass[...] = jnp.zeros(mass.shape, jnp.float32)
    turned = jnp.transpose(g_ref[...])
    for q in range(slots):
        spread[q] = jnp.broadcast_to(turned[:, q : q + 1], (points, 128))

    @pl.loop(0, blocks * slots)
    def _(unit):
        r = unit // slots
        q = unit % slots

        @pl.when(live[unit] > 0)
        def _():
            bias = spread[q]
            bias = jnp.concatenate([bias] * (tile // 128), axis=1)
            for start in range(0, rows, tile):
                scores = lax.dot_general(
                    t_ref[q],
                    s_ref[r, start : start + tile],
                    (((1,), (1,)), ((), ())),
                    preferred_element_type=jnp.float32,
                )
                absorb(scores + bias, peak, mass, (r, slice(None), slice(start, start + tile)))

    for r in range(blocks):
        out[r : r + 1, :] = collapse(peak[r], mass[r])


def row_pass(live, rows_all, target, shifted):
    blocks, rows, _ = rows_all.shape
    slots, points, _ = target.shape
    return pl.pallas_call(
        row_kernel,
        out_shape=jax.ShapeDtypeStruct((blocks, rows), jnp.float32),
        in_specs=[sspec(), vspec(), vspec(), vspec()],
        out_specs=vspec(),
        scratch_shapes=[
            VMEM((blocks, 8, rows), jnp.float32),
            VMEM((blocks, 8, rows), jnp.float32),
            VMEM((slots, points, 128), jnp.float32),
        ],
        compiler_params=pltpu.CompilerParams(vmem_limit_bytes=LIMIT),
        name="row_pass",
    )(live, rows_all, target, shifted)


def column_kernel(live, s_ref, t_ref, r_ref, out, peak, mass, spread):
    blocks, rows, depth = s_ref.shape
    slots, points, _ = t_ref.shape
    tile = tile_of(rows)
    peak[...] = jnp.full(peak.shape, FLOOR_VALUE, jnp.float32)
    mass[...] = jnp.zeros(mass.shape, jnp.float32)
    turned = jnp.transpose(r_ref[...])
    for r in range(blocks):
        spread[r] = jnp.broadcast_to(turned[:, r : r + 1], (rows, 128))

    @pl.loop(0, blocks * slots)
    def _(unit):
        r = unit // slots
        q = unit % slots

        @pl.when(live[unit] > 0)
        def _():
            for start in range(0, rows, tile):
                bias = spread[r, start : start + tile]
                bias = jnp.concatenate([bias] * (points // 128), axis=1)
                scores = lax.dot_general(
                    s_ref[r, start : start + tile],
                    t_ref[q],
                    (((1,), (1,)), ((), ())),
                    preferred_element_type=jnp.float32,
                )
                absorb(scores - bias, peak, mass, (q,))

    for q in range(slots):
        out[q : q + 1, :] = collapse(peak[q], mass[q])


def column_pass(live, rows_all, target, row_log):
    blocks, rows, _ = rows_all.shape
    slots, points, _ = target.shape
    return pl.pallas_call(
        column_kernel,
        out_shape=jax.ShapeDtypeStruct((slots, points), jnp.float32),
        in_specs=[sspec(), vspec(), vspec(), vspec()],
        out_specs=vspec(),
        scratch_shapes=[
            VMEM((slots, 8, points), jnp.float32),
            VMEM((slots, 8, points), jnp.float32),
            VMEM((blocks, rows, 128), jnp.float32),
        ],
        compiler_params=pltpu.CompilerParams(vmem_limit_bytes=LIMIT),
        name="column_pass",
    )(live, rows_all, target, row_log)


def join_kernel(sizes, sign, x_ref, out, held, send, recv):
    names = list(sizes)
    total = math.prod(sizes.values())
    place = {n: lax.axis_index(n) for n in names}

    def peer(offset):
        ident = {}
        rest = offset
        for n in reversed(names):
            ident[n] = lax.rem(place[n] + rest % sizes[n], sizes[n])
            rest = rest // sizes[n]
        return ident

    barrier = pltpu.get_barrier_semaphore()
    for offset in range(1, total):
        pl.semaphore_signal(barrier, inc=1, device_id=peer(offset), device_id_type=MESH)
    pl.semaphore_wait(barrier, total - 1)
    copies = []
    for offset in range(1, total):
        copy = pltpu.make_async_remote_copy(
            src_ref=x_ref,
            dst_ref=held.at[offset - 1],
            send_sem=send.at[offset - 1],
            recv_sem=recv.at[offset - 1],
            device_id=peer(offset),
            device_id_type=MESH,
        )
        copy.start()
        copies.append(copy)
    for copy in copies:
        copy.wait()
    out[...] = sign * log_sum([x_ref[...]] + [held[i] for i in range(total - 1)])


def join_logs(x, sizes, ident, sign):
    total = math.prod(sizes.values())
    return pl.pallas_call(
        functools.partial(join_kernel, sizes, sign),
        out_shape=jax.ShapeDtypeStruct(x.shape, jnp.float32),
        in_specs=[vspec()],
        out_specs=vspec(),
        scratch_shapes=[
            VMEM((total - 1,) + x.shape, jnp.float32),
            pltpu.SemaphoreType.DMA((total - 1,)),
            pltpu.SemaphoreType.DMA((total - 1,)),
        ],
        compiler_params=pltpu.CompilerParams(
            collective_id=ident, has_side_effects=True, vmem_limit_bytes=LIMIT
        ),
        name="join_" + "_".join(sizes),
    )(x)


def per_device(source, target, target_slot_index, active_block_table, active_count):
    blocks = lax.axis_size("blk")
    own_index = lax.axis_index("blk")
    source_rows = source[0]
    slots = target.shape[0]
    listlen = active_block_table.shape[1]
    names = jnp.arange(target_slot_index.shape[0], dtype=jnp.int32)
    table_matches = active_block_table[:, :, None] == names[None, None, :]
    slot_table = jnp.sum(jnp.where(table_matches, target_slot_index[None, None, :], 0), axis=2)
    live_mask = jnp.arange(listlen, dtype=jnp.int32)[None, :] < active_count[:, None]
    own_slots = own_index * slots + jnp.arange(slots, dtype=jnp.int32)
    live = jnp.any(
        live_mask[:, :, None] & (slot_table[:, :, None] == own_slots[None, None, :]), axis=1
    )
    named = jnp.any(live, axis=0)
    live_units = live.reshape(-1).astype(jnp.int32)
    half_rows = 0.5 * jnp.sum(jnp.square(source_rows.astype(jnp.float32)), axis=1)
    half_cols = 0.5 * jnp.sum(jnp.square(target.astype(jnp.float32)), axis=2)

    across = {"blk": blocks, "pair": lax.axis_size("pair")}
    along = {"sub": lax.axis_size("sub")}
    rows_all = gather_rows(source_rows, blocks)
    shifted = -half_cols
    for _ in range(ITERS):
        row_log = join_logs(row_pass(live_units, rows_all, target, shifted), across, 1, 1.0)
        shifted = join_logs(column_pass(live_units, rows_all, target, row_log), along, 2, -1.0)
    own_log = lax.dynamic_index_in_dim(row_log, own_index, 0, keepdims=False)
    row_pot = half_rows - own_log
    potential = jnp.where(named[:, None], half_cols + shifted, 0.0)
    return (row_pot[None, :], potential)


def solution(mesh):
    placed = (
        P(("groups", "blk"), "sub", None),
        P(("groups", "blk"), "pair", None),
        P("groups"),
        P("groups", None),
        P("groups"),
    )
    return jax.shard_map(
        per_device,
        mesh=mesh,
        in_specs=placed,
        out_specs=(P(("groups", "blk"), "sub"), P(("groups", "blk"), "pair")),
        check_vma=False,
    )
```

```python
import functools
import math

import jax
import jax.numpy as jnp
from jax import lax
from jax.experimental import pallas as pl
from jax.experimental.pallas import tpu as pltpu
from jax.sharding import PartitionSpec as P

ITERS = 3
EPSILON = 0.01
FLOOR_VALUE = -1e30
TO_BITS = 1.0 / (EPSILON * math.log(2.0))
FROM_BITS = EPSILON * math.log(2.0)
MESH = pl.DeviceIdType.MESH
LIMIT = 48 * 1024 * 1024
VMEM = pltpu.VMEM


def vspec():
    return pl.BlockSpec(memory_space=pltpu.VMEM)


def sspec():
    return pl.BlockSpec(memory_space=pltpu.SMEM)


def log_join(peak, mass):
    safe = jnp.where(mass > 0.0, mass, 1.0)
    return jnp.where(mass > 0.0, peak + FROM_BITS * jnp.log2(safe), FLOOR_VALUE)


def log_sum(parts):
    peak = functools.reduce(jnp.maximum, parts)
    mass = functools.reduce(jnp.add, [jnp.exp2((p - peak) * TO_BITS) for p in parts])
    return peak + FROM_BITS * jnp.log2(mass)


def collapse(peak, mass):
    top = jnp.max(peak, axis=0, keepdims=True)
    total = jnp.sum(mass * jnp.exp2((peak - top) * TO_BITS), axis=0, keepdims=True)
    return log_join(top, total)


def gather_kernel(blocks, s_ref, all_ref, up_send, up_recv, down_send, down_recv, pair_send, pair_recv, own_sem):
    z = lax.axis_index("blk")
    c = lax.axis_index("pair")
    rows = s_ref.shape[0]
    half = rows // 2
    mine = pl.ds(pl.multiple_of(c * half, half), half)
    barrier = pltpu.get_barrier_semaphore()
    has_up = z + 1 < blocks
    has_down = z > 0

    @pl.when(has_up)
    def _():
        pl.semaphore_signal(barrier, inc=1, device_id={"blk": z + 1}, device_id_type=MESH)

    @pl.when(has_down)
    def _():
        pl.semaphore_signal(barrier, inc=1, device_id={"blk": z - 1}, device_id_type=MESH)

    pl.semaphore_signal(barrier, inc=1, device_id={"pair": 1 - c}, device_id_type=MESH)
    pl.semaphore_wait(barrier, 1 + has_up.astype(jnp.int32) + has_down.astype(jnp.int32))

    def hop(block, step, target, send, recv, first):
        return pltpu.make_async_remote_copy(
            src_ref=s_ref.at[mine] if first else all_ref.at[block, mine],
            dst_ref=all_ref.at[block, mine],
            send_sem=send.at[step],
            recv_sem=recv.at[step],
            device_id={"blk": target},
            device_id_type=MESH,
        )

    def across(block, slot):
        return pltpu.make_async_remote_copy(
            src_ref=all_ref.at[block, mine],
            dst_ref=all_ref.at[block, mine],
            send_sem=pair_send.at[slot],
            recv_sem=pair_recv.at[slot],
            device_id={"pair": 1 - c},
            device_id_type=MESH,
        )

    own = pltpu.make_async_copy(s_ref, all_ref.at[z], own_sem)
    own.start()

    @pl.when(has_up)
    def _():
        hop(z, 0, z + 1, up_send, up_recv, True).start()

    @pl.when(has_down)
    def _():
        hop(z, 0, z - 1, down_send, down_recv, True).start()

    for step in range(blocks - 1):
        below = z - 1 - step
        above = z + 1 + step

        @pl.when(below >= 0)
        def _():
            hop(below, step, z, up_send, up_recv, False).wait_recv()

            @pl.when(has_up)
            def _():
                hop(below, step + 1, z + 1, up_send, up_recv, False).start()

            across(below, below).start()

        @pl.when(above < blocks)
        def _():
            hop(above, step, z, down_send, down_recv, False).wait_recv()

            @pl.when(has_down)
            def _():
                hop(above, step + 1, z - 1, down_send, down_recv, False).start()

            across(above, above).start()

    own.wait()
    for block in range(blocks):

        @pl.when(block != z)
        def _():
            across(block, block).wait()

    for step in range(blocks):

        @pl.when(has_up & (z - step >= 0))
        def _():
            hop(z, step, z + 1, up_send, up_recv, True).wait_send()

        @pl.when(has_down & (z + step < blocks))
        def _():
            hop(z, step, z - 1, down_send, down_recv, True).wait_send()


def gather_rows(source, blocks):
    return pl.pallas_call(
        functools.partial(gather_kernel, blocks),
        out_shape=jax.ShapeDtypeStruct((blocks,) + source.shape, source.dtype),
        in_specs=[vspec()],
        out_specs=vspec(),
        scratch_shapes=[pltpu.SemaphoreType.DMA((blocks,)) for _ in range(6)]
        + [pltpu.SemaphoreType.DMA],
        compiler_params=pltpu.CompilerParams(
            collective_id=0, has_side_effects=True, vmem_limit_bytes=LIMIT
        ),
        name="gather_rows",
    )(source)


def tile_of(rows):
    return 256 if rows % 256 == 0 else rows


def absorb(scores, peak, mass, at):
    parts = scores.reshape(scores.shape[0] // 8, 8, scores.shape[1])
    old = peak[at]
    new = jnp.maximum(old, jnp.max(parts, axis=0))
    peak[at] = new
    mass[at] = mass[at] * jnp.exp2((old - new) * TO_BITS) + jnp.sum(
        jnp.exp2((parts - new[None]) * TO_BITS), axis=0
    )


def row_kernel(live, s_ref, t_ref, g_ref, out, peak, mass, spread):
    blocks, rows, depth = s_ref.shape
    slots, points, _ = t_ref.shape
    tile = tile_of(rows)
    peak[...] = jnp.full(peak.shape, FLOOR_VALUE, jnp.float32)
    mass[...] = jnp.zeros(mass.shape, jnp.float32)
    turned = jnp.transpose(g_ref[...])
    for q in range(slots):
        spread[q] = jnp.broadcast_to(turned[:, q : q + 1], (points, 128))

    @pl.loop(0, blocks * slots)
    def _(unit):
        r = unit // slots
        q = unit % slots

        @pl.when(live[unit] > 0)
        def _():
            bias = spread[q]
            bias = jnp.concatenate([bias] * (tile // 128), axis=1)
            for start in range(0, rows, tile):
                scores = lax.dot_general(
                    t_ref[q],
                    s_ref[r, start : start + tile],
                    (((1,), (1,)), ((), ())),
                    preferred_element_type=jnp.float32,
                )
                absorb(scores + bias, peak, mass, (r, slice(None), slice(start, start + tile)))

    for r in range(blocks):
        out[r : r + 1, :] = collapse(peak[r], mass[r])


def row_pass(live, rows_all, target, shifted):
    blocks, rows, _ = rows_all.shape
    slots, points, _ = target.shape
    return pl.pallas_call(
        row_kernel,
        out_shape=jax.ShapeDtypeStruct((blocks, rows), jnp.float32),
        in_specs=[sspec(), vspec(), vspec(), vspec()],
        out_specs=vspec(),
        scratch_shapes=[
            VMEM((blocks, 8, rows), jnp.float32),
            VMEM((blocks, 8, rows), jnp.float32),
            VMEM((slots, points, 128), jnp.float32),
        ],
        compiler_params=pltpu.CompilerParams(vmem_limit_bytes=LIMIT),
        name="row_pass",
    )(live, rows_all, target, shifted)


def column_kernel(live, s_ref, t_ref, r_ref, out, peak, mass, spread):
    blocks, rows, depth = s_ref.shape
    slots, points, _ = t_ref.shape
    tile = tile_of(rows)
    peak[...] = jnp.full(peak.shape, FLOOR_VALUE, jnp.float32)
    mass[...] = jnp.zeros(mass.shape, jnp.float32)
    turned = jnp.transpose(r_ref[...])
    for r in range(blocks):
        spread[r] = jnp.broadcast_to(turned[:, r : r + 1], (rows, 128))

    @pl.loop(0, blocks * slots)
    def _(unit):
        r = unit // slots
        q = unit % slots

        @pl.when(live[unit] > 0)
        def _():
            for start in range(0, rows, tile):
                bias = spread[r, start : start + tile]
                bias = jnp.concatenate([bias] * (points // 128), axis=1)
                scores = lax.dot_general(
                    s_ref[r, start : start + tile],
                    t_ref[q],
                    (((1,), (1,)), ((), ())),
                    preferred_element_type=jnp.float32,
                )
                absorb(scores - bias, peak, mass, (q,))

    for q in range(slots):
        out[q : q + 1, :] = collapse(peak[q], mass[q])


def column_pass(live, rows_all, target, row_log):
    blocks, rows, _ = rows_all.shape
    slots, points, _ = target.shape
    return pl.pallas_call(
        column_kernel,
        out_shape=jax.ShapeDtypeStruct((slots, points), jnp.float32),
        in_specs=[sspec(), vspec(), vspec(), vspec()],
        out_specs=vspec(),
        scratch_shapes=[
            VMEM((slots, 8, points), jnp.float32),
            VMEM((slots, 8, points), jnp.float32),
            VMEM((blocks, rows, 128), jnp.float32),
        ],
        compiler_params=pltpu.CompilerParams(vmem_limit_bytes=LIMIT),
        name="column_pass",
    )(live, rows_all, target, row_log)


def join_kernel(sizes, sign, x_ref, out, held, send, recv):
    names = list(sizes)
    total = math.prod(sizes.values())
    place = {n: lax.axis_index(n) for n in names}

    def peer(offset):
        ident = {}
        rest = offset
        for n in reversed(names):
            ident[n] = lax.rem(place[n] + rest % sizes[n], sizes[n])
            rest = rest // sizes[n]
        return ident

    barrier = pltpu.get_barrier_semaphore()
    for offset in range(1, total):
        pl.semaphore_signal(barrier, inc=1, device_id=peer(offset), device_id_type=MESH)
    pl.semaphore_wait(barrier, total - 1)
    copies = []
    for offset in range(1, total):
        copy = pltpu.make_async_remote_copy(
            src_ref=x_ref,
            dst_ref=held.at[offset - 1],
            send_sem=send.at[offset - 1],
            recv_sem=recv.at[offset - 1],
            device_id=peer(offset),
            device_id_type=MESH,
        )
        copy.start()
        copies.append(copy)
    for copy in copies:
        copy.wait()
    out[...] = sign * log_sum([x_ref[...]] + [held[i] for i in range(total - 1)])


def join_logs(x, sizes, ident, sign):
    total = math.prod(sizes.values())
    return pl.pallas_call(
        functools.partial(join_kernel, sizes, sign),
        out_shape=jax.ShapeDtypeStruct(x.shape, jnp.float32),
        in_specs=[vspec()],
        out_specs=vspec(),
        scratch_shapes=[
            VMEM((total - 1,) + x.shape, jnp.float32),
            pltpu.SemaphoreType.DMA((total - 1,)),
            pltpu.SemaphoreType.DMA((total - 1,)),
        ],
        compiler_params=pltpu.CompilerParams(
            collective_id=ident, has_side_effects=True, vmem_limit_bytes=LIMIT
        ),
        name="join_" + "_".join(sizes),
    )(x)


def fused_kernel(
    sizes, live, s_ref, t_ref, hs_ref, ht_ref, row_out, col_out,
    scores, rows_all, spread, row_mine, row_held, row_log, col_mine, col_held, columns,
    up_send, up_recv, down_send, down_recv, pair_send, pair_recv,
    row_send, row_recv, col_send, col_recv,
):
    blocks = sizes["blk"]
    z = lax.axis_index("blk")
    c = lax.axis_index("pair")
    rows = s_ref.shape[0]
    slots, points, _ = t_ref.shape
    half = rows // 2
    mine = pl.ds(pl.multiple_of(c * half, half), half)
    across_names = {"blk": blocks, "pair": sizes["pair"]}
    across_count = blocks * sizes["pair"]
    sub_count = sizes["sub"]

    def peer(offset):
        return {
            "blk": lax.rem(z + offset // sizes["pair"], blocks),
            "pair": lax.rem(c + offset % sizes["pair"], sizes["pair"]),
        }

    def side(offset):
        return {"sub": lax.rem(lax.axis_index("sub") + offset, sub_count)}

    barrier = pltpu.get_barrier_semaphore()
    for offset in range(1, across_count):
        pl.semaphore_signal(barrier, inc=1, device_id=peer(offset), device_id_type=MESH)
    for offset in range(1, sub_count):
        pl.semaphore_signal(barrier, inc=1, device_id=side(offset), device_id_type=MESH)
    pl.semaphore_wait(barrier, across_count + sub_count - 2)
    has_up = z + 1 < blocks
    has_down = z > 0

    def hop(block, step, target, send, recv, first):
        return pltpu.make_async_remote_copy(
            src_ref=s_ref.at[mine] if first else rows_all.at[block, mine],
            dst_ref=rows_all.at[block, mine],
            send_sem=send.at[step],
            recv_sem=recv.at[step],
            device_id={"blk": target},
            device_id_type=MESH,
        )

    def across(block):
        return pltpu.make_async_remote_copy(
            src_ref=rows_all.at[block, mine],
            dst_ref=rows_all.at[block, mine],
            send_sem=pair_send.at[block],
            recv_sem=pair_recv.at[block],
            device_id={"pair": 1 - c},
            device_id_type=MESH,
        )

    def fill(block, load):
        @pl.loop(0, slots)
        def _(q):
            shut = jnp.where(live[block * slots + q] > 0, 0.0, FLOOR_VALUE)
            for start in range(0, rows, 256):
                value = lax.dot_general(
                    t_ref[q],
                    load(start),
                    (((1,), (1,)), ((), ())),
                    preferred_element_type=jnp.float32,
                )
                scores[block, q, :, start : start + 256] = value * TO_BITS + shut

    @pl.when(has_up)
    def _():
        hop(z, 0, z + 1, up_send, up_recv, True).start()

    @pl.when(has_down)
    def _():
        hop(z, 0, z - 1, down_send, down_recv, True).start()

    turned = jnp.transpose(ht_ref[...]) * (-TO_BITS)
    for q in range(slots):
        spread[q] = jnp.broadcast_to(turned[:, q : q + 1], (points, 128))
    fill(z, lambda start: s_ref[start : start + 256])

    for step in range(blocks - 1):
        below = z - 1 - step
        above = z + 1 + step

        @pl.when(below >= 0)
        def _():
            hop(below, step, z, up_send, up_recv, False).wait_recv()

            @pl.when(has_up)
            def _():
                hop(below, step + 1, z + 1, up_send, up_recv, False).start()

            across(below).start()

        @pl.when(above < blocks)
        def _():
            hop(above, step, z, down_send, down_recv, False).wait_recv()

            @pl.when(has_down)
            def _():
                hop(above, step + 1, z - 1, down_send, down_recv, False).start()

            across(above).start()

        @pl.when(below >= 0)
        def _():
            across(below).wait_recv()
            fill(below, lambda start: rows_all[below, start : start + 256])

        @pl.when(above < blocks)
        def _():
            across(above).wait_recv()
            fill(above, lambda start: rows_all[above, start : start + 256])

    for iteration in range(ITERS):

        @pl.loop(0, blocks)
        def _(r):
            for start in range(0, rows, 256):
                span = slice(start, start + 256)
                peak = None
                for q in range(slots):
                    bias = jnp.concatenate([spread[q]] * 2, axis=1)
                    value = (scores[r, q, :, span] + bias).reshape(points // 8, 8, 256)
                    top = jnp.max(value, axis=0)
                    peak = top if peak is None else jnp.maximum(peak, top)
                mass = jnp.zeros((8, 256), jnp.float32)
                for q in range(slots):
                    bias = jnp.concatenate([spread[q]] * 2, axis=1)
                    value = (scores[r, q, :, span] + bias).reshape(points // 8, 8, 256)
                    mass = mass + jnp.sum(jnp.exp2(value - peak[None]), axis=0)
                top = jnp.max(peak, axis=0, keepdims=True)
                total = jnp.sum(mass * jnp.exp2(peak - top), axis=0, keepdims=True)
                row_mine[iteration, pl.ds(r, 1), span] = top + jnp.log2(total)

        copies = []
        for offset in range(1, across_count):
            copy = pltpu.make_async_remote_copy(
                src_ref=row_mine.at[iteration],
                dst_ref=row_held.at[iteration, offset - 1],
                send_sem=row_send.at[iteration, offset - 1],
                recv_sem=row_recv.at[iteration, offset - 1],
                device_id=peer(offset),
                device_id_type=MESH,
            )
            copy.start()
            copies.append(copy)
        for copy in copies:
            copy.wait()
        parts = [row_mine[iteration]] + [row_held[iteration, i] for i in range(across_count - 1)]
        row_log[...] = bit_sum(parts)

        for q in range(slots):

            @pl.loop(0, points // 64)
            def _(piece):
                part = pl.ds(pl.multiple_of(piece * 64, 64), 64)
                peak = jnp.full((64, 128), FLOOR_VALUE, jnp.float32)
                for r in range(blocks):
                    for start in range(0, rows, 128):
                        span = slice(start, start + 128)
                        peak = jnp.maximum(peak, scores[r, q, part, span] - row_log[r : r + 1, span])
                mass = jnp.zeros((64, 128), jnp.float32)
                for r in range(blocks):
                    for start in range(0, rows, 128):
                        span = slice(start, start + 128)
                        value = scores[r, q, part, span] - row_log[r : r + 1, span]
                        mass = mass + jnp.exp2(value - peak)
                top = jnp.max(peak, axis=1, keepdims=True)
                total = jnp.sum(mass * jnp.exp2(peak - top), axis=1, keepdims=True)
                columns[part, q : q + 1] = top + jnp.log2(total)

        col_mine[iteration] = jnp.transpose(columns[...])
        copies = []
        for offset in range(1, sub_count):
            copy = pltpu.make_async_remote_copy(
                src_ref=col_mine.at[iteration],
                dst_ref=col_held.at[iteration, offset - 1],
                send_sem=col_send.at[iteration, offset - 1],
                recv_sem=col_recv.at[iteration, offset - 1],
                device_id=side(offset),
                device_id_type=MESH,
            )
            copy.start()
            copies.append(copy)
        for copy in copies:
            copy.wait()
        total = bit_sum(
            [col_mine[iteration]] + [col_held[iteration, i] for i in range(sub_count - 1)]
        )
        named = total > 0.1 * FLOOR_VALUE
        shifted = jnp.where(named, -total, 0.0)
        if iteration < ITERS - 1:
            turned = jnp.transpose(shifted)
            for q in range(slots):
                spread[q] = jnp.broadcast_to(turned[:, q : q + 1], (points, 128))
        else:
            col_out[...] = jnp.where(named, ht_ref[...] + FROM_BITS * shifted, 0.0)

    row_out[...] = hs_ref[...] - FROM_BITS * row_log[pl.ds(z, 1), :]

    for block in range(blocks):

        @pl.when(block != z)
        def _():
            across(block).wait_send()

    for step in range(blocks):

        @pl.when(has_up & (z - step >= 0))
        def _():
            hop(z, step, z + 1, up_send, up_recv, True).wait_send()

        @pl.when(has_down & (z + step < blocks))
        def _():
            hop(z, step, z - 1, down_send, down_recv, True).wait_send()


def bit_sum(parts):
    peak = functools.reduce(jnp.maximum, parts)
    mass = functools.reduce(jnp.add, [jnp.exp2(p - peak) for p in parts])
    return peak + jnp.log2(mass)


def fused(live, source_rows, target, half_rows, half_cols, sizes):
    rows = source_rows.shape[0]
    slots, points, _ = target.shape
    blocks = sizes["blk"]
    peers = blocks * sizes["pair"] - 1
    sides = sizes["sub"] - 1
    dma = pltpu.SemaphoreType.DMA
    return pl.pallas_call(
        functools.partial(fused_kernel, sizes),
        out_shape=(
            jax.ShapeDtypeStruct((1, rows), jnp.float32),
            jax.ShapeDtypeStruct((slots, points), jnp.float32),
        ),
        in_specs=[sspec(), vspec(), vspec(), vspec(), vspec()],
        out_specs=(vspec(), vspec()),
        scratch_shapes=[
            VMEM((blocks, slots, points, rows), jnp.float32),
            VMEM((blocks,) + source_rows.shape, source_rows.dtype),
            VMEM((slots, points, 128), jnp.float32),
            VMEM((ITERS, blocks, rows), jnp.float32),
            VMEM((ITERS, peers, blocks, rows), jnp.float32),
            VMEM((blocks, rows), jnp.float32),
            VMEM((ITERS, slots, points), jnp.float32),
            VMEM((ITERS, sides, slots, points), jnp.float32),
            VMEM((points, slots), jnp.float32),
        ]
        + [dma((blocks,)) for _ in range(6)]
        + [dma((ITERS, peers)), dma((ITERS, peers)), dma((ITERS, sides)), dma((ITERS, sides))],
        compiler_params=pltpu.CompilerParams(
            collective_id=3, has_side_effects=True, vmem_limit_bytes=56 * 1024 * 1024
        ),
        name="fused_sinkhorn",
    )(live, source_rows, target, half_rows, half_cols)


def per_device(source, target, target_slot_index, active_block_table, active_count):
    blocks = lax.axis_size("blk")
    own_index = lax.axis_index("blk")
    source_rows = source[0]
    slots = target.shape[0]
    listlen = active_block_table.shape[1]
    names = jnp.arange(target_slot_index.shape[0], dtype=jnp.int32)
    table_matches = active_block_table[:, :, None] == names[None, None, :]
    slot_table = jnp.sum(jnp.where(table_matches, target_slot_index[None, None, :], 0), axis=2)
    live_mask = jnp.arange(listlen, dtype=jnp.int32)[None, :] < active_count[:, None]
    own_slots = own_index * slots + jnp.arange(slots, dtype=jnp.int32)
    live = jnp.any(
        live_mask[:, :, None] & (slot_table[:, :, None] == own_slots[None, None, :]), axis=1
    )
    named = jnp.any(live, axis=0)
    live_units = live.reshape(-1).astype(jnp.int32)
    half_rows = 0.5 * jnp.sum(jnp.square(source_rows.astype(jnp.float32)), axis=1)
    half_cols = 0.5 * jnp.sum(jnp.square(target.astype(jnp.float32)), axis=2)

    rows = source_rows.shape[0]
    sizes = {n: lax.axis_size(n) for n in ("blk", "sub", "pair")}
    held_bytes = 4 * blocks * rows * slots * target.shape[1]
    if held_bytes <= 32 * 1024 * 1024 and rows % 512 == 0 and sizes["pair"] == 2:
        return fused(live_units, source_rows, target, half_rows[None, :], half_cols, sizes)

    across = {"blk": blocks, "pair": lax.axis_size("pair")}
    along = {"sub": lax.axis_size("sub")}
    rows_all = gather_rows(source_rows, blocks)
    shifted = -half_cols
    for _ in range(ITERS):
        row_log = join_logs(row_pass(live_units, rows_all, target, shifted), across, 1, 1.0)
        shifted = join_logs(column_pass(live_units, rows_all, target, row_log), along, 2, -1.0)
    own_log = lax.dynamic_index_in_dim(row_log, own_index, 0, keepdims=False)
    row_pot = half_rows - own_log
    potential = jnp.where(named[:, None], half_cols + shifted, 0.0)
    return (row_pot[None, :], potential)


def solution(mesh):
    placed = (
        P(("groups", "blk"), "sub", None),
        P(("groups", "blk"), "pair", None),
        P("groups"),
        P("groups", None),
        P("groups"),
    )
    return jax.shard_map(
        per_device,
        mesh=mesh,
        in_specs=placed,
        out_specs=(P(("groups", "blk"), "sub"), P(("groups", "blk"), "pair")),
        check_vma=False,
    )
```

```python
import functools
import math

import jax
import jax.numpy as jnp
from jax import lax
from jax.experimental import pallas as pl
from jax.experimental.pallas import tpu as pltpu
from jax.sharding import PartitionSpec as P

ITERS = 3
EPSILON = 0.01
FLOOR_VALUE = -1e30
TO_BITS = 1.0 / (EPSILON * math.log(2.0))
FROM_BITS = EPSILON * math.log(2.0)
MESH = pl.DeviceIdType.MESH
LIMIT = 48 * 1024 * 1024
VMEM = pltpu.VMEM


def vspec():
    return pl.BlockSpec(memory_space=pltpu.VMEM)


def sspec():
    return pl.BlockSpec(memory_space=pltpu.SMEM)


def log_join(peak, mass):
    safe = jnp.where(mass > 0.0, mass, 1.0)
    return jnp.where(mass > 0.0, peak + FROM_BITS * jnp.log2(safe), FLOOR_VALUE)


def log_sum(parts):
    peak = functools.reduce(jnp.maximum, parts)
    mass = functools.reduce(jnp.add, [jnp.exp2((p - peak) * TO_BITS) for p in parts])
    return peak + FROM_BITS * jnp.log2(mass)


def collapse(peak, mass):
    top = jnp.max(peak, axis=0, keepdims=True)
    total = jnp.sum(mass * jnp.exp2((peak - top) * TO_BITS), axis=0, keepdims=True)
    return log_join(top, total)


def gather_kernel(blocks, s_ref, all_ref, up_send, up_recv, down_send, down_recv, pair_send, pair_recv, own_sem):
    z = lax.axis_index("blk")
    c = lax.axis_index("pair")
    rows = s_ref.shape[0]
    half = rows // 2
    mine = pl.ds(pl.multiple_of(c * half, half), half)
    barrier = pltpu.get_barrier_semaphore()
    has_up = z + 1 < blocks
    has_down = z > 0

    @pl.when(has_up)
    def _():
        pl.semaphore_signal(barrier, inc=1, device_id={"blk": z + 1}, device_id_type=MESH)

    @pl.when(has_down)
    def _():
        pl.semaphore_signal(barrier, inc=1, device_id={"blk": z - 1}, device_id_type=MESH)

    pl.semaphore_signal(barrier, inc=1, device_id={"pair": 1 - c}, device_id_type=MESH)
    pl.semaphore_wait(barrier, 1 + has_up.astype(jnp.int32) + has_down.astype(jnp.int32))

    def hop(block, step, target, send, recv, first):
        return pltpu.make_async_remote_copy(
            src_ref=s_ref.at[mine] if first else all_ref.at[block, mine],
            dst_ref=all_ref.at[block, mine],
            send_sem=send.at[step],
            recv_sem=recv.at[step],
            device_id={"blk": target},
            device_id_type=MESH,
        )

    def across(block, slot):
        return pltpu.make_async_remote_copy(
            src_ref=all_ref.at[block, mine],
            dst_ref=all_ref.at[block, mine],
            send_sem=pair_send.at[slot],
            recv_sem=pair_recv.at[slot],
            device_id={"pair": 1 - c},
            device_id_type=MESH,
        )

    own = pltpu.make_async_copy(s_ref, all_ref.at[z], own_sem)
    own.start()

    @pl.when(has_up)
    def _():
        hop(z, 0, z + 1, up_send, up_recv, True).start()

    @pl.when(has_down)
    def _():
        hop(z, 0, z - 1, down_send, down_recv, True).start()

    for step in range(blocks - 1):
        below = z - 1 - step
        above = z + 1 + step

        @pl.when(below >= 0)
        def _():
            hop(below, step, z, up_send, up_recv, False).wait_recv()

            @pl.when(has_up)
            def _():
                hop(below, step + 1, z + 1, up_send, up_recv, False).start()

            across(below, below).start()

        @pl.when(above < blocks)
        def _():
            hop(above, step, z, down_send, down_recv, False).wait_recv()

            @pl.when(has_down)
            def _():
                hop(above, step + 1, z - 1, down_send, down_recv, False).start()

            across(above, above).start()

    own.wait()
    for block in range(blocks):

        @pl.when(block != z)
        def _():
            across(block, block).wait()

    for step in range(blocks):

        @pl.when(has_up & (z - step >= 0))
        def _():
            hop(z, step, z + 1, up_send, up_recv, True).wait_send()

        @pl.when(has_down & (z + step < blocks))
        def _():
            hop(z, step, z - 1, down_send, down_recv, True).wait_send()


def gather_rows(source, blocks):
    return pl.pallas_call(
        functools.partial(gather_kernel, blocks),
        out_shape=jax.ShapeDtypeStruct((blocks,) + source.shape, source.dtype),
        in_specs=[vspec()],
        out_specs=vspec(),
        scratch_shapes=[pltpu.SemaphoreType.DMA((blocks,)) for _ in range(6)]
        + [pltpu.SemaphoreType.DMA],
        compiler_params=pltpu.CompilerParams(
            collective_id=0, has_side_effects=True, vmem_limit_bytes=LIMIT
        ),
        name="gather_rows",
    )(source)


def tile_of(rows):
    return 256 if rows % 256 == 0 else rows


def absorb(scores, peak, mass, at):
    parts = scores.reshape(scores.shape[0] // 8, 8, scores.shape[1])
    old = peak[at]
    new = jnp.maximum(old, jnp.max(parts, axis=0))
    peak[at] = new
    mass[at] = mass[at] * jnp.exp2((old - new) * TO_BITS) + jnp.sum(
        jnp.exp2((parts - new[None]) * TO_BITS), axis=0
    )


def row_kernel(live, s_ref, t_ref, g_ref, out, peak, mass, spread):
    blocks, rows, depth = s_ref.shape
    slots, points, _ = t_ref.shape
    tile = tile_of(rows)
    peak[...] = jnp.full(peak.shape, FLOOR_VALUE, jnp.float32)
    mass[...] = jnp.zeros(mass.shape, jnp.float32)
    turned = jnp.transpose(g_ref[...])
    for q in range(slots):
        spread[q] = jnp.broadcast_to(turned[:, q : q + 1], (points, 128))

    @pl.loop(0, blocks * slots)
    def _(unit):
        r = unit // slots
        q = unit % slots

        @pl.when(live[unit] > 0)
        def _():
            bias = spread[q]
            bias = jnp.concatenate([bias] * (tile // 128), axis=1)
            for start in range(0, rows, tile):
                scores = lax.dot_general(
                    t_ref[q],
                    s_ref[r, start : start + tile],
                    (((1,), (1,)), ((), ())),
                    preferred_element_type=jnp.float32,
                )
                absorb(scores + bias, peak, mass, (r, slice(None), slice(start, start + tile)))

    for r in range(blocks):
        out[r : r + 1, :] = collapse(peak[r], mass[r])


def row_pass(live, rows_all, target, shifted):
    blocks, rows, _ = rows_all.shape
    slots, points, _ = target.shape
    return pl.pallas_call(
        row_kernel,
        out_shape=jax.ShapeDtypeStruct((blocks, rows), jnp.float32),
        in_specs=[sspec(), vspec(), vspec(), vspec()],
        out_specs=vspec(),
        scratch_shapes=[
            VMEM((blocks, 8, rows), jnp.float32),
            VMEM((blocks, 8, rows), jnp.float32),
            VMEM((slots, points, 128), jnp.float32),
        ],
        compiler_params=pltpu.CompilerParams(vmem_limit_bytes=LIMIT),
        name="row_pass",
    )(live, rows_all, target, shifted)


def column_kernel(live, s_ref, t_ref, r_ref, out, peak, mass, spread):
    blocks, rows, depth = s_ref.shape
    slots, points, _ = t_ref.shape
    tile = tile_of(rows)
    peak[...] = jnp.full(peak.shape, FLOOR_VALUE, jnp.float32)
    mass[...] = jnp.zeros(mass.shape, jnp.float32)
    turned = jnp.transpose(r_ref[...])
    for r in range(blocks):
        spread[r] = jnp.broadcast_to(turned[:, r : r + 1], (rows, 128))

    @pl.loop(0, blocks * slots)
    def _(unit):
        r = unit // slots
        q = unit % slots

        @pl.when(live[unit] > 0)
        def _():
            for start in range(0, rows, tile):
                bias = spread[r, start : start + tile]
                bias = jnp.concatenate([bias] * (points // 128), axis=1)
                scores = lax.dot_general(
                    s_ref[r, start : start + tile],
                    t_ref[q],
                    (((1,), (1,)), ((), ())),
                    preferred_element_type=jnp.float32,
                )
                absorb(scores - bias, peak, mass, (q,))

    for q in range(slots):
        out[q : q + 1, :] = collapse(peak[q], mass[q])


def column_pass(live, rows_all, target, row_log):
    blocks, rows, _ = rows_all.shape
    slots, points, _ = target.shape
    return pl.pallas_call(
        column_kernel,
        out_shape=jax.ShapeDtypeStruct((slots, points), jnp.float32),
        in_specs=[sspec(), vspec(), vspec(), vspec()],
        out_specs=vspec(),
        scratch_shapes=[
            VMEM((slots, 8, points), jnp.float32),
            VMEM((slots, 8, points), jnp.float32),
            VMEM((blocks, rows, 128), jnp.float32),
        ],
        compiler_params=pltpu.CompilerParams(vmem_limit_bytes=LIMIT),
        name="column_pass",
    )(live, rows_all, target, row_log)


def join_kernel(sizes, sign, x_ref, out, held, send, recv):
    names = list(sizes)
    total = math.prod(sizes.values())
    place = {n: lax.axis_index(n) for n in names}

    def peer(offset):
        ident = {}
        rest = offset
        for n in reversed(names):
            ident[n] = lax.rem(place[n] + rest % sizes[n], sizes[n])
            rest = rest // sizes[n]
        return ident

    barrier = pltpu.get_barrier_semaphore()
    for offset in range(1, total):
        pl.semaphore_signal(barrier, inc=1, device_id=peer(offset), device_id_type=MESH)
    pl.semaphore_wait(barrier, total - 1)
    copies = []
    for offset in range(1, total):
        copy = pltpu.make_async_remote_copy(
            src_ref=x_ref,
            dst_ref=held.at[offset - 1],
            send_sem=send.at[offset - 1],
            recv_sem=recv.at[offset - 1],
            device_id=peer(offset),
            device_id_type=MESH,
        )
        copy.start()
        copies.append(copy)
    for copy in copies:
        copy.wait()
    out[...] = sign * log_sum([x_ref[...]] + [held[i] for i in range(total - 1)])


def join_logs(x, sizes, ident, sign):
    total = math.prod(sizes.values())
    return pl.pallas_call(
        functools.partial(join_kernel, sizes, sign),
        out_shape=jax.ShapeDtypeStruct(x.shape, jnp.float32),
        in_specs=[vspec()],
        out_specs=vspec(),
        scratch_shapes=[
            VMEM((total - 1,) + x.shape, jnp.float32),
            pltpu.SemaphoreType.DMA((total - 1,)),
            pltpu.SemaphoreType.DMA((total - 1,)),
        ],
        compiler_params=pltpu.CompilerParams(
            collective_id=ident, has_side_effects=True, vmem_limit_bytes=LIMIT
        ),
        name="join_" + "_".join(sizes),
    )(x)


def fused_kernel(
    sizes, live, s_ref, t_ref, hs_ref, ht_ref, row_out, col_out,
    scores, rows_all, spread, row_mine, row_held, row_log, col_mine, col_held, columns,
    up_send, up_recv, down_send, down_recv, pair_send, pair_recv,
    row_send, row_recv, col_send, col_recv,
):
    blocks = sizes["blk"]
    z = lax.axis_index("blk")
    c = lax.axis_index("pair")
    rows = s_ref.shape[0]
    slots, points, _ = t_ref.shape
    half = rows // 2
    mine = pl.ds(pl.multiple_of(c * half, half), half)
    across_names = {"blk": blocks, "pair": sizes["pair"]}
    across_count = blocks * sizes["pair"]
    sub_count = sizes["sub"]

    def peer(offset):
        return {
            "blk": lax.rem(z + offset // sizes["pair"], blocks),
            "pair": lax.rem(c + offset % sizes["pair"], sizes["pair"]),
        }

    def side(offset):
        return {"sub": lax.rem(lax.axis_index("sub") + offset, sub_count)}

    barrier = pltpu.get_barrier_semaphore()
    for offset in range(1, across_count):
        pl.semaphore_signal(barrier, inc=1, device_id=peer(offset), device_id_type=MESH)
    for offset in range(1, sub_count):
        pl.semaphore_signal(barrier, inc=1, device_id=side(offset), device_id_type=MESH)
    pl.semaphore_wait(barrier, across_count + sub_count - 2)
    has_up = z + 1 < blocks
    has_down = z > 0

    def hop(block, step, target, send, recv, first):
        return pltpu.make_async_remote_copy(
            src_ref=s_ref.at[mine] if first else rows_all.at[block, mine],
            dst_ref=rows_all.at[block, mine],
            send_sem=send.at[step],
            recv_sem=recv.at[step],
            device_id={"blk": target},
            device_id_type=MESH,
        )

    def across(block):
        return pltpu.make_async_remote_copy(
            src_ref=rows_all.at[block, mine],
            dst_ref=rows_all.at[block, mine],
            send_sem=pair_send.at[block],
            recv_sem=pair_recv.at[block],
            device_id={"pair": 1 - c},
            device_id_type=MESH,
        )

    def fill(block, load):
        @pl.loop(0, slots)
        def _(q):
            shut = jnp.where(live[block * slots + q] > 0, 0.0, FLOOR_VALUE)
            for start in range(0, rows, 256):
                value = lax.dot_general(
                    t_ref[q],
                    load(start),
                    (((1,), (1,)), ((), ())),
                    preferred_element_type=jnp.float32,
                )
                scores[block, q, :, start : start + 256] = value * TO_BITS + shut

    def row_update(iteration, r):
        for start in range(0, rows, 512):
            span = slice(start, start + 512)
            peak = jnp.full((8, 512), FLOOR_VALUE, jnp.float32)
            mass = jnp.zeros((8, 512), jnp.float32)
            for q in range(slots):
                bias = jnp.concatenate([spread[q]] * 4, axis=1)
                value = (scores[r, q, :, span] + bias).reshape(points // 8, 8, 512)
                newer = jnp.maximum(peak, jnp.max(value, axis=0))
                mass = mass * jnp.exp2(peak - newer) + jnp.sum(
                    jnp.exp2(value - newer[None]), axis=0
                )
                peak = newer
            top = jnp.max(peak, axis=0, keepdims=True)
            total = jnp.sum(mass * jnp.exp2(peak - top), axis=0, keepdims=True)
            row_mine[iteration, pl.ds(r, 1), span] = top + jnp.log2(total)

    @pl.when(has_up)
    def _():
        hop(z, 0, z + 1, up_send, up_recv, True).start()

    @pl.when(has_down)
    def _():
        hop(z, 0, z - 1, down_send, down_recv, True).start()

    turned = jnp.transpose(ht_ref[...]) * (-TO_BITS)
    for q in range(slots):
        spread[q] = jnp.broadcast_to(turned[:, q : q + 1], (points, 128))
    columns[...] = jnp.zeros(columns.shape, jnp.float32)
    fill(z, lambda start: s_ref[start : start + 256])
    row_update(0, z)

    @pl.loop(0, blocks - 1)
    def _(step):
        below = z - 1 - step
        above = z + 1 + step

        @pl.when(below >= 0)
        def _():
            hop(below, step, z, up_send, up_recv, False).wait_recv()

            @pl.when(has_up)
            def _():
                hop(below, step + 1, z + 1, up_send, up_recv, False).start()

            across(below).start()

        @pl.when(above < blocks)
        def _():
            hop(above, step, z, down_send, down_recv, False).wait_recv()

            @pl.when(has_down)
            def _():
                hop(above, step + 1, z - 1, down_send, down_recv, False).start()

            across(above).start()

        for block, there in ((below, below >= 0), (above, above < blocks)):

            @pl.when(there)
            def _():
                across(block).wait_recv()
                fill(block, lambda start: rows_all[block, start : start + 256])
                row_update(0, block)

    lanes = lax.broadcasted_iota(jnp.int32, (points, 128), 1)

    @pl.loop(0, ITERS)
    def _(iteration):
        copies = []
        for offset in range(1, across_count):
            copy = pltpu.make_async_remote_copy(
                src_ref=row_mine.at[iteration],
                dst_ref=row_held.at[iteration, offset - 1],
                send_sem=row_send.at[iteration, offset - 1],
                recv_sem=row_recv.at[iteration, offset - 1],
                device_id=peer(offset),
                device_id_type=MESH,
            )
            copy.start()
            copies.append(copy)
        for copy in copies:
            copy.wait()
        parts = [row_mine[iteration]] + [row_held[iteration, i] for i in range(across_count - 1)]
        row_log[...] = bit_sum(parts)

        @pl.loop(0, slots)
        def _(q):
            peak = jnp.full((points, 128), FLOOR_VALUE, jnp.float32)
            mass = jnp.zeros((points, 128), jnp.float32)
            for r in range(blocks):
                for base in range(0, rows, 1024):
                    values = [
                        scores[r, q, :, start : start + 128] - row_log[r : r + 1, start : start + 128]
                        for start in range(base, min(base + 1024, rows), 128)
                    ]
                    newer = functools.reduce(jnp.maximum, values, peak)
                    mass = mass * jnp.exp2(peak - newer)
                    for value in values:
                        mass = mass + jnp.exp2(value - newer)
                    peak = newer
            top = jnp.max(peak, axis=1, keepdims=True)
            total = jnp.sum(mass * jnp.exp2(peak - top), axis=1, keepdims=True)
            columns[...] = jnp.where(lanes == q, top + jnp.log2(total), columns[...])

        col_mine[iteration] = jnp.transpose(columns[:, 0:slots])
        copies = []
        for offset in range(1, sub_count):
            copy = pltpu.make_async_remote_copy(
                src_ref=col_mine.at[iteration],
                dst_ref=col_held.at[iteration, offset - 1],
                send_sem=col_send.at[iteration, offset - 1],
                recv_sem=col_recv.at[iteration, offset - 1],
                device_id=side(offset),
                device_id_type=MESH,
            )
            copy.start()
            copies.append(copy)
        for copy in copies:
            copy.wait()
        total = bit_sum(
            [col_mine[iteration]] + [col_held[iteration, i] for i in range(sub_count - 1)]
        )
        named = total > 0.1 * FLOOR_VALUE
        shifted = jnp.where(named, -total, 0.0)
        col_out[...] = jnp.where(named, ht_ref[...] + FROM_BITS * shifted, 0.0)

        @pl.when(iteration < ITERS - 1)
        def _():
            turned = jnp.transpose(shifted)
            for q in range(slots):
                spread[q] = jnp.broadcast_to(turned[:, q : q + 1], (points, 128))

            @pl.loop(0, blocks)
            def _(r):
                row_update(iteration + 1, r)

    row_out[...] = hs_ref[...] - FROM_BITS * row_log[pl.ds(z, 1), :]

    for block in range(blocks):

        @pl.when(block != z)
        def _():
            across(block).wait_send()

    for step in range(blocks):

        @pl.when(has_up & (z - step >= 0))
        def _():
            hop(z, step, z + 1, up_send, up_recv, True).wait_send()

        @pl.when(has_down & (z + step < blocks))
        def _():
            hop(z, step, z - 1, down_send, down_recv, True).wait_send()


def bit_sum(parts):
    peak = functools.reduce(jnp.maximum, parts)
    mass = functools.reduce(jnp.add, [jnp.exp2(p - peak) for p in parts])
    return peak + jnp.log2(mass)


def fused(live, source_rows, target, half_rows, half_cols, sizes):
    rows = source_rows.shape[0]
    slots, points, _ = target.shape
    blocks = sizes["blk"]
    peers = blocks * sizes["pair"] - 1
    sides = sizes["sub"] - 1
    dma = pltpu.SemaphoreType.DMA
    return pl.pallas_call(
        functools.partial(fused_kernel, sizes),
        out_shape=(
            jax.ShapeDtypeStruct((1, rows), jnp.float32),
            jax.ShapeDtypeStruct((slots, points), jnp.float32),
        ),
        in_specs=[sspec(), vspec(), vspec(), vspec(), vspec()],
        out_specs=(vspec(), vspec()),
        scratch_shapes=[
            VMEM((blocks, slots, points, rows), jnp.float32),
            VMEM((blocks,) + source_rows.shape, source_rows.dtype),
            VMEM((slots, points, 128), jnp.float32),
            VMEM((ITERS, blocks, rows), jnp.float32),
            VMEM((ITERS, peers, blocks, rows), jnp.float32),
            VMEM((blocks, rows), jnp.float32),
            VMEM((ITERS, slots, points), jnp.float32),
            VMEM((ITERS, sides, slots, points), jnp.float32),
            VMEM((points, 128), jnp.float32),
        ]
        + [dma((blocks,)) for _ in range(6)]
        + [dma((ITERS, peers)), dma((ITERS, peers)), dma((ITERS, sides)), dma((ITERS, sides))],
        compiler_params=pltpu.CompilerParams(
            collective_id=3, has_side_effects=True, vmem_limit_bytes=56 * 1024 * 1024
        ),
        name="fused_sinkhorn",
    )(live, source_rows, target, half_rows, half_cols)


def per_device(source, target, target_slot_index, active_block_table, active_count):
    blocks = lax.axis_size("blk")
    own_index = lax.axis_index("blk")
    source_rows = source[0]
    slots = target.shape[0]
    listlen = active_block_table.shape[1]
    names = jnp.arange(target_slot_index.shape[0], dtype=jnp.int32)
    table_matches = active_block_table[:, :, None] == names[None, None, :]
    slot_table = jnp.sum(jnp.where(table_matches, target_slot_index[None, None, :], 0), axis=2)
    live_mask = jnp.arange(listlen, dtype=jnp.int32)[None, :] < active_count[:, None]
    own_slots = own_index * slots + jnp.arange(slots, dtype=jnp.int32)
    live = jnp.any(
        live_mask[:, :, None] & (slot_table[:, :, None] == own_slots[None, None, :]), axis=1
    )
    named = jnp.any(live, axis=0)
    live_units = live.reshape(-1).astype(jnp.int32)
    half_rows = 0.5 * jnp.sum(jnp.square(source_rows.astype(jnp.float32)), axis=1)
    half_cols = 0.5 * jnp.sum(jnp.square(target.astype(jnp.float32)), axis=2)

    rows = source_rows.shape[0]
    sizes = {n: lax.axis_size(n) for n in ("blk", "sub", "pair")}
    held_bytes = 4 * blocks * rows * slots * target.shape[1]
    if held_bytes <= 32 * 1024 * 1024 and rows % 512 == 0 and sizes["pair"] == 2:
        return fused(live_units, source_rows, target, half_rows[None, :], half_cols, sizes)

    across = {"blk": blocks, "pair": lax.axis_size("pair")}
    along = {"sub": lax.axis_size("sub")}
    rows_all = gather_rows(source_rows, blocks)
    shifted = -half_cols
    for _ in range(ITERS):
        row_log = join_logs(row_pass(live_units, rows_all, target, shifted), across, 1, 1.0)
        shifted = join_logs(column_pass(live_units, rows_all, target, row_log), along, 2, -1.0)
    own_log = lax.dynamic_index_in_dim(row_log, own_index, 0, keepdims=False)
    row_pot = half_rows - own_log
    potential = jnp.where(named[:, None], half_cols + shifted, 0.0)
    return (row_pot[None, :], potential)


def solution(mesh):
    placed = (
        P(("groups", "blk"), "sub", None),
        P(("groups", "blk"), "pair", None),
        P("groups"),
        P("groups", None),
        P("groups"),
    )
    return jax.shard_map(
        per_device,
        mesh=mesh,
        in_specs=placed,
        out_specs=(P(("groups", "blk"), "sub"), P(("groups", "blk"), "pair")),
        check_vma=False,
    )
```
